32 devices in a mesh: seq: 8 (over z, core), tensor: 4 (over y, x).
Axes of the slice: x: 2, y: 2, z: 4, core: 2. Of those that a mesh axis runs over, the one named last changes fastest.
Arguments:
- queries: bfloat16 [6144, 4096], P('seq', 'tensor'), may hold values from -12 to 12
- keys: bfloat16 [6144, 1024], P('seq', 'tensor'), may hold values from -12 to 12
- values: bfloat16 [6144, 1024], P('seq', 'tensor'), may hold values from -6 to 6
- out_weight: bfloat16 [4096, 4096], P('tensor'), may hold values from -0.09375 to 0.09375
- out_grad: bfloat16 [6144, 4096], P('seq', 'tensor'), may hold values from -6 to 6
- doc_ids: int32 [6144], P('seq'), may hold values from 0 to 3, never falling along the last dimension, each value on 1 to 3072 neighbouring positions
Outputs:
- grad_queries: bfloat16 [6144, 4096], P('seq', 'tensor')
- grad_keys: bfloat16 [6144, 1024], P('seq', 'tensor')
- grad_values: bfloat16 [6144, 1024], P('seq', 'tensor')
- grad_out_weight: bfloat16 [4096, 4096], P('tensor', 'seq')
The draws below stay inside these ranges and needn't reach their ends.
Inputs may be any that keep to these rules, and one draw needn't show every extreme that they name: `doc_ids`: document numbers never fall along the sequence; a document holds 1 to 3072 tokens and one holds exactly that many.
All inputs are finite; a program needn't handle non-finite values.
Results may differ from the reference program's by a relative error of at most 0.015.
Values may be sent and summed in bfloat16 or wider, within the bound.
A program may use at most 192 MiB of HBM per device.

```python
import math
import jax
import jax.numpy as jnp
import numpy as np
from jax import lax

D = 4096
QUERY_HEADS = 32
KEY_VALUE_HEADS = 8
HEAD_SIZE = 128
TOKENS_PER_SHARD = 768
SEQUENCE_TOKENS = 6144
WINDOW = 1536
DOCS = 4
N_SEQ = 8


def draw_queries(key, part):
    newest_part = jax.random.fold_in(key, 13)
    return jnp.clip(jax.random.normal(newest_part, (SEQUENCE_TOKENS, QUERY_HEADS * HEAD_SIZE), jnp.float32), -6.0, 6.0).astype(jnp.bfloat16)


def draw_keys(key, part):
    newest_part = jax.random.fold_in(key, 12)
    return jnp.clip(2.0 * jax.random.normal(newest_part, (SEQUENCE_TOKENS, KEY_VALUE_HEADS * HEAD_SIZE), jnp.float32), -12.0, 12.0).astype(jnp.bfloat16)


def raised(result, stream_key, source, target, blocks, factor):
    owner, partner = [(jnp.arange(result.shape[dim]) // (result.shape[dim] // blocks)).reshape([-1 if axis == dim else 1 for axis in range(result.ndim)]) for dim in (source, target)]
    chosen = jax.random.permutation(stream_key, blocks)[partner]
    strong = (owner == chosen) | (owner == (partner + blocks // 2) % blocks)
    return jnp.where(strong, factor * result, result)


def shard_levels(own_key, shape, split, smallest, high):
    loudness = 1.0
    for axis_at, blocks in split:
        heights = jax.random.uniform(jax.random.fold_in(jax.random.fold_in(own_key, 6), axis_at), (blocks,), jnp.float32, smallest / len(split), high / len(split))
        loudness = loudness * jnp.repeat(jnp.exp(heights), shape[axis_at] // blocks).reshape((-1,) + (1,) * (len(shape) - 1 - axis_at))
    return loudness


def split_up(number_of, total, limit, slope):
    weights = [(1 << 20) // math.isqrt(standing ** slope) + 1 for standing in range(2, number_of + 1)]
    surplus, given = total - limit - (number_of - 1), [1] * (number_of - 1)
    while surplus > 0:
        candidates = [i for i in range(number_of - 1) if given[i] < limit]
        mass, budget = sum([weights[i] for i in candidates]), surplus
        for i in candidates:
            addition = min(limit - given[i], max(1, budget * weights[i] // mass), surplus)
            given[i] = given[i] + addition
            surplus = surplus - addition
    return np.array([limit] + given)


def ragged_sizes(own_key, amount, total, reach, skew):
    if amount == 2:
        one = jax.random.randint(own_key, (), max(1, total - reach), min(reach, total - 1) + 1)
        return jnp.stack([one, total - one])
    lengths = jnp.asarray(split_up(amount, total, reach, skew), jnp.int32)
    pairs = (amount - 1) // 2
    source_of, taker = lengths[1:1 + 2 * pairs:2], lengths[2:2 + 2 * pairs:2]
    margin = jnp.minimum(source_of - 1, reach - taker)
    passed = jax.random.randint(jax.random.fold_in(own_key, 1), (pairs,), 0, 1 << 20) % (margin + 1)
    lengths = lengths.at[1:1 + 2 * pairs:2].set(source_of - passed).at[2:2 + 2 * pairs:2].set(taker + passed)
    return lengths[jax.random.permutation(jax.random.fold_in(own_key, 2), amount)]


def bell_draw(own_key, shape, deviation, bound, split=(), kind=jnp.bfloat16):
    array = jax.random.normal(own_key, shape, jnp.float32) * deviation
    if len(split) > 0:
        array = shard_levels(own_key, shape, split, -0.22, 0.18) * array
    return jnp.clip(array, min=-bound, max=bound).astype(kind)


def bell_draw_with(key, dims, scale, bound, pieces, heavy, held_as=jnp.bfloat16):
    array = scale * jax.random.normal(key, dims, jnp.float32)
    if pieces:
        array = array * shard_levels(key, dims, pieces, -0.22, 0.18)
    return jnp.clip(raised(array, jax.random.fold_in(key, 3), *heavy), -bound, bound).astype(held_as)


def setup_inputs(seed: int = 0) -> dict:
    streams_of = jax.random.split(jax.random.key(seed), 7)
    return {
        "queries": draw_queries(jax.random.fold_in(streams_of[6], 71), 0),
        "keys": draw_keys(jax.random.fold_in(streams_of[6], 71), 0),
        "values": bell_draw(streams_of[2], (SEQUENCE_TOKENS, KEY_VALUE_HEADS * HEAD_SIZE), 1.0, 6.0, ((0, 8), (1, 4))),
        "out_weight": bell_draw(streams_of[3], (QUERY_HEADS * HEAD_SIZE, D), (QUERY_HEADS * HEAD_SIZE) ** -0.5, 0.09375, ((0, 4),)),
        "out_grad": bell_draw_with(streams_of[4], (SEQUENCE_TOKENS, D), 1.0, 6.0, ((0, 8), (1, 4)), (0, 1, 8, 2.0)),
        "doc_ids": jnp.searchsorted(jnp.cumsum(ragged_sizes(streams_of[5], DOCS, SEQUENCE_TOKENS, 4 * TOKENS_PER_SHARD, 1)), jnp.arange(SEQUENCE_TOKENS), side="right").astype(jnp.int32),
    }


NEG_BIG = -1e+30

def reference(queries, keys, values, out_weight, out_grad, doc_ids):
    group_factor = QUERY_HEADS // KEY_VALUE_HEADS
    scale = 1.0 / math.sqrt(HEAD_SIZE)
    attention_gradient = jnp.dot(out_grad, out_weight.T, preferred_element_type=jnp.float32).astype(jnp.bfloat16)
    padded_keys = jnp.concatenate([jnp.zeros((2 * TOKENS_PER_SHARD, KEY_VALUE_HEADS * HEAD_SIZE), keys.dtype), keys], axis=0)
    padded_values = jnp.concatenate([jnp.zeros((2 * TOKENS_PER_SHARD, KEY_VALUE_HEADS * HEAD_SIZE), values.dtype), values], axis=0)
    pad_docs = jnp.concatenate([jnp.zeros((2 * TOKENS_PER_SHARD,), jnp.int32), doc_ids.astype(jnp.int32)])

    def block(index):
        start_index = (index * TOKENS_PER_SHARD).astype(jnp.int32)
        query_block = lax.dynamic_slice_in_dim(queries, start_index, TOKENS_PER_SHARD, 0).astype(jnp.float32).reshape(TOKENS_PER_SHARD, KEY_VALUE_HEADS, group_factor, HEAD_SIZE)
        key_block = lax.dynamic_slice_in_dim(padded_keys, start_index, 3 * TOKENS_PER_SHARD, 0).astype(jnp.float32).reshape(3 * TOKENS_PER_SHARD, KEY_VALUE_HEADS, HEAD_SIZE)
        value_block = lax.dynamic_slice_in_dim(padded_values, start_index, 3 * TOKENS_PER_SHARD, 0).astype(jnp.float32).reshape(3 * TOKENS_PER_SHARD, KEY_VALUE_HEADS, HEAD_SIZE)
        doc_q = lax.dynamic_slice_in_dim(doc_ids.astype(jnp.int32), start_index, TOKENS_PER_SHARD, 0)
        doc_k = lax.dynamic_slice_in_dim(pad_docs, start_index, 3 * TOKENS_PER_SHARD, 0)
        block_gradient = lax.dynamic_slice_in_dim(attention_gradient, start_index, TOKENS_PER_SHARD, 0).astype(jnp.float32).reshape(TOKENS_PER_SHARD, KEY_VALUE_HEADS, group_factor, HEAD_SIZE)
        q_pos = start_index + jnp.arange(TOKENS_PER_SHARD, dtype=jnp.int32)
        k_pos = start_index - 2 * TOKENS_PER_SHARD + jnp.arange(3 * TOKENS_PER_SHARD, dtype=jnp.int32)
        gap = q_pos[:, None] - k_pos[None, :]
        visible = (gap >= 0) & (gap < WINDOW) & (k_pos[None, :] >= 0) & (doc_q[:, None] == doc_k[None, :])
        raw = jnp.einsum('qgeh,kgh->geqk', query_block, key_block) * scale
        masked = jnp.where(visible, raw, NEG_BIG)
        top = lax.optimization_barrier(jnp.max(masked, axis=-1, keepdims=True))
        expo = jnp.where(visible, jnp.exp(masked - top), 0.0)
        probs = expo / lax.optimization_barrier(jnp.sum(expo, axis=-1, keepdims=True))
        probs_low = lax.optimization_barrier(probs.astype(jnp.bfloat16)).astype(jnp.float32)
        attention_output = jnp.einsum('geqk,kgh->qgeh', probs_low, value_block).astype(jnp.bfloat16)
        attn_wide = lax.optimization_barrier(attention_output).astype(jnp.float32)
        delta = jnp.transpose(lax.optimization_barrier(jnp.sum(block_gradient * attn_wide, axis=-1)), (1, 2, 0))[..., None]
        d_prob = jnp.einsum('qgeh,kgh->geqk', block_gradient, value_block)
        d_score = lax.optimization_barrier((probs * (d_prob - delta)).astype(jnp.bfloat16)).astype(jnp.float32)
        query_gradient = (jnp.einsum('geqk,kgh->qgeh', d_score, key_block) * scale).astype(jnp.bfloat16)
        key_gradient = jnp.einsum('geqk,qgeh->kgh', d_score, query_block) * scale
        value_gradient = jnp.einsum('geqk,qgeh->kgh', probs_low, block_gradient)
        return (attention_output.reshape(TOKENS_PER_SHARD, QUERY_HEADS * HEAD_SIZE), query_gradient.reshape(TOKENS_PER_SHARD, QUERY_HEADS * HEAD_SIZE), key_gradient.reshape(3, TOKENS_PER_SHARD, KEY_VALUE_HEADS * HEAD_SIZE), value_gradient.reshape(3, TOKENS_PER_SHARD, KEY_VALUE_HEADS * HEAD_SIZE))
    attention_output, query_gradient, k_parts, v_parts = lax.map(block, jnp.arange(N_SEQ, dtype=jnp.int32))

    def combine(part_count):
        first_zeros = jnp.zeros((1, TOKENS_PER_SHARD, KEY_VALUE_HEADS * HEAD_SIZE), jnp.float32)
        second_zeros = jnp.zeros((2, TOKENS_PER_SHARD, KEY_VALUE_HEADS * HEAD_SIZE), jnp.float32)
        nearby_part = jnp.concatenate([part_count[1:, 1], first_zeros], axis=0)
        distant_part = jnp.concatenate([part_count[2:, 0], second_zeros], axis=0)
        return (part_count[:, 2] + nearby_part + distant_part).reshape(SEQUENCE_TOKENS, KEY_VALUE_HEADS * HEAD_SIZE).astype(jnp.bfloat16)
    attention_output = attention_output.reshape(SEQUENCE_TOKENS, QUERY_HEADS * HEAD_SIZE)
    grad_w = lax.dot_general(attention_output, out_grad, (((0,), (0,)), ((), ())), preferred_element_type=jnp.float32)
    return (query_gradient.reshape(SEQUENCE_TOKENS, QUERY_HEADS * HEAD_SIZE), combine(k_parts), combine(v_parts), grad_w.astype(jnp.bfloat16))
```

```python
import functools
import math

import jax
import jax.numpy as jnp
from jax import lax
from jax.experimental import pallas as pl
from jax.experimental.pallas import tpu as pltpu
from jax.sharding import PartitionSpec as P

HEAD_SIZE = 128
TILE = 256
NEG_BIG = -1e30
VMEM_BYTES = 50 * 1024 * 1024


def mm(left, right, left_dim, right_dim):
    return lax.dot_general(
        left, right, (((left_dim,), (right_dim,)), ((), ())), preferred_element_type=jnp.float32
    )


def params(count):
    return pltpu.CompilerParams(
        dimension_semantics=("arbitrary",) * count, vmem_limit_bytes=VMEM_BYTES
    )


def lane_heads(ref, factor):
    return jnp.concatenate(
        [ref[:, h * HEAD_SIZE : (h + 1) * HEAD_SIZE] for h in range(factor)], axis=0
    )


def assemble(target, parts, tok):
    for index, part in enumerate(parts):
        target[index * tok : (index + 1) * tok, :] = part[...]


def visible_tile(limit, j, last):
    rows = lax.broadcasted_iota(jnp.int32, (TILE, TILE), 0)
    seen = rows >= limit - j * TILE
    if j == last:
        seen = seen & (rows <= lax.broadcasted_iota(jnp.int32, (TILE, TILE), 1))
    return seen


def forward_kernel(
    tok, factor, low_ref, q_ref, kd, kn, ko, vd, vn, vo, attn_ref, lse_ref, k_scr, v_scr, vt_scr
):
    step = pl.program_id(1)
    scale = math.log2(math.e) / math.sqrt(HEAD_SIZE)

    @pl.when(step == 0)
    def _():
        assemble(k_scr, (kd, kn, ko), tok)
        assemble(v_scr, (vd, vn, vo), tok)
        vt_scr[...] = v_scr[...].T

    tiles = 2 * tok // TILE + 1
    base = pl.multiple_of(step * TILE, TILE)
    limit = low_ref[...] - base
    for h in range(factor):
        q_head = q_ref[:, h * HEAD_SIZE : (h + 1) * HEAD_SIZE]
        scores = []
        top = None
        for j in range(tiles):
            k_tile = k_scr[pl.ds(pl.multiple_of(base + j * TILE, TILE), TILE), :]
            raw = mm(k_tile, q_head, 1, 1)
            raw = jnp.where(visible_tile(limit, j, tiles - 1), raw, NEG_BIG)
            scores.append(raw)
            high = jnp.max(raw, axis=0, keepdims=True)
            top = high if top is None else jnp.maximum(top, high)
        shift = top * scale
        total = None
        low_parts = []
        for j in range(tiles):
            expo = jnp.exp2(scores[j] * scale - shift)
            part = jnp.sum(expo, axis=0, keepdims=True)
            total = part if total is None else total + part
            low_parts.append(expo.astype(jnp.bfloat16))
        weights = jnp.concatenate(low_parts, axis=0)
        vt = vt_scr[:, pl.ds(base, tiles * TILE)]
        out_t = mm(vt, weights, 1, 0) / total
        attn_ref[:, h * HEAD_SIZE : (h + 1) * HEAD_SIZE] = out_t.T.astype(jnp.bfloat16)
        lse_ref[0, h : h + 1, :] = shift + jnp.log2(total)


def backward_kernel(
    tok, factor, low_ref, lse_ref, q_ref, do_ref, at_ref, kd, kn, ko, vd, vn, vo,
    dq_ref, own_ref, far_ref, k_scr, v_scr, kt_scr, dk_scr, dv_scr, dq_scr,
):
    step = pl.program_id(0)
    scale = math.log2(math.e) / math.sqrt(HEAD_SIZE)
    plain = 1.0 / math.sqrt(HEAD_SIZE)

    @pl.when(step == 0)
    def _():
        assemble(k_scr, (kd, kn, ko), tok)
        assemble(v_scr, (vd, vn, vo), tok)
        kt_scr[...] = k_scr[...].T
        dk_scr[...] = jnp.zeros_like(dk_scr)
        dv_scr[...] = jnp.zeros_like(dv_scr)

    tiles = 2 * tok // TILE + 1
    base = pl.multiple_of(step * TILE, TILE)
    limit = low_ref[...] - base
    q_stack = lane_heads(q_ref, factor)
    do_stack = lane_heads(do_ref, factor)
    at_stack = lane_heads(at_ref, factor)
    product = do_stack.astype(jnp.float32) * at_stack.astype(jnp.float32)
    delta = jnp.sum(product.T, axis=0, keepdims=True)
    for j in range(tiles):
        rows = pl.ds(pl.multiple_of(base + j * TILE, TILE), TILE)
        k_tile = k_scr[rows, :]
        v_tile = v_scr[rows, :]
        seen = visible_tile(limit, j, tiles - 1)
        probs_parts = []
        score_parts = []
        for h in range(factor):
            part = slice(h * TILE, (h + 1) * TILE)
            raw = mm(k_tile, q_stack[part], 1, 1)
            d_prob = mm(v_tile, do_stack[part], 1, 1)
            probs = jnp.exp2(raw * scale - lse_ref[0, h : h + 1, :])
            probs = jnp.where(seen, probs, 0.0)
            probs_parts.append(probs.astype(jnp.bfloat16))
            score_parts.append((probs * (d_prob - delta[:, part])).astype(jnp.bfloat16))
        probs_all = jnp.concatenate(probs_parts, axis=1)
        score_all = jnp.concatenate(score_parts, axis=1)
        dv_scr[rows, :] += mm(probs_all, do_stack, 1, 0)
        dk_scr[rows, :] += mm(score_all, q_stack, 1, 0)
        kt = kt_scr[:, pl.ds(pl.multiple_of(base + j * TILE, TILE), TILE)]
        gain = mm(kt, score_all, 1, 0)
        if j == 0:
            dq_scr[...] = gain
        else:
            dq_scr[...] += gain
    for h in range(factor):
        piece = dq_scr[:, h * TILE : (h + 1) * TILE] * plain
        dq_ref[:, h * HEAD_SIZE : (h + 1) * HEAD_SIZE] = piece.T.astype(jnp.bfloat16)

    @pl.when(step == pl.num_programs(0) - 1)
    def _():
        own_ref[:, :HEAD_SIZE] = dk_scr[2 * tok :, :] * plain
        own_ref[:, HEAD_SIZE:] = dv_scr[2 * tok :, :]
        far_ref[:, :HEAD_SIZE] = (dk_scr[: 2 * tok, :] * plain).astype(jnp.bfloat16)
        far_ref[:, HEAD_SIZE:] = dv_scr[: 2 * tok, :].astype(jnp.bfloat16)


def key_specs(tok, kv_heads, column):
    specs = []
    for offset in (0, kv_heads):
        for _ in range(3):
            specs.append(
                pl.BlockSpec((tok, HEAD_SIZE), functools.partial(column, offset))
            )
    return specs


def forward(low, queries, kv, tok, kv_heads, factor):
    tiles = 2 * tok // TILE + 1
    flops = 4 * tok * tiles * TILE * HEAD_SIZE * kv_heads * factor
    return pl.pallas_call(
        functools.partial(forward_kernel, tok, factor),
        grid=(kv_heads, tok // TILE),
        in_specs=[
            pl.BlockSpec((1, TILE), lambda g, i: (0, i)),
            pl.BlockSpec((TILE, factor * HEAD_SIZE), lambda g, i: (i, g)),
        ]
        + key_specs(tok, kv_heads, lambda offset, g, i: (0, g + offset)),
        out_specs=[
            pl.BlockSpec((TILE, factor * HEAD_SIZE), lambda g, i: (i, g)),
            pl.BlockSpec((1, factor, TILE), lambda g, i: (g, 0, i)),
        ],
        out_shape=[
            jax.ShapeDtypeStruct(queries.shape, jnp.bfloat16),
            jax.ShapeDtypeStruct((kv_heads, factor, tok), jnp.float32),
        ],
        scratch_shapes=[
            pltpu.VMEM((3 * tok, HEAD_SIZE), jnp.bfloat16),
            pltpu.VMEM((3 * tok, HEAD_SIZE), jnp.bfloat16),
            pltpu.VMEM((HEAD_SIZE, 3 * tok), jnp.bfloat16),
        ],
        compiler_params=params(2),
        cost_estimate=pl.CostEstimate(
            flops=4 * flops, bytes_accessed=8 * 2**20, transcendentals=0
        ),
        name="attention_forward",
    )(low, queries, *(kv * 2))


def backward(group, low, lse, queries, d_attn, attn, kv, tok, kv_heads, factor):
    tiles = 2 * tok // TILE + 1
    flops = 10 * tok * tiles * TILE * HEAD_SIZE * factor
    wide = pl.BlockSpec((TILE, factor * HEAD_SIZE), lambda i: (i, group))
    whole = lambda i: (0, 0)
    return pl.pallas_call(
        functools.partial(backward_kernel, tok, factor),
        grid=(tok // TILE,),
        in_specs=[
            pl.BlockSpec((1, TILE), lambda i: (0, i)),
            pl.BlockSpec((1, factor, TILE), lambda i: (group, 0, i)),
            wide,
            wide,
            wide,
        ]
        + key_specs(tok, kv_heads, lambda offset, i: (0, group + offset)),
        out_specs=[
            pl.BlockSpec((TILE, factor * HEAD_SIZE), lambda i: (i, 0)),
            pl.BlockSpec((tok, 2 * HEAD_SIZE), whole),
            pl.BlockSpec((2 * tok, 2 * HEAD_SIZE), whole),
        ],
        out_shape=[
            jax.ShapeDtypeStruct((tok, factor * HEAD_SIZE), jnp.bfloat16),
            jax.ShapeDtypeStruct((tok, 2 * HEAD_SIZE), jnp.float32),
            jax.ShapeDtypeStruct((2 * tok, 2 * HEAD_SIZE), jnp.bfloat16),
        ],
        scratch_shapes=[
            pltpu.VMEM((3 * tok, HEAD_SIZE), jnp.bfloat16),
            pltpu.VMEM((3 * tok, HEAD_SIZE), jnp.bfloat16),
            pltpu.VMEM((HEAD_SIZE, 3 * tok), jnp.bfloat16),
            pltpu.VMEM((3 * tok, HEAD_SIZE), jnp.float32),
            pltpu.VMEM((3 * tok, HEAD_SIZE), jnp.float32),
            pltpu.VMEM((HEAD_SIZE, factor * TILE), jnp.float32),
        ],
        compiler_params=params(1),
        cost_estimate=pl.CostEstimate(
            flops=3 * flops, bytes_accessed=8 * 2**20, transcendentals=0
        ),
        name="attention_backward",
    )(low, lse, queries, d_attn, attn, *(kv * 2))


def project_kernel(g_ref, w_ref, out_ref, acc):
    step = pl.program_id(0)
    gain = mm(g_ref[0], w_ref[...], 1, 1)

    @pl.when(step == 0)
    def _():
        acc[...] = gain

    @pl.when(step > 0)
    def _():
        acc[...] += gain

    @pl.when(step == pl.num_programs(0) - 1)
    def _():
        out_ref[...] = acc[...].astype(jnp.bfloat16)


def project(grads, out_weight):
    count, tok, width = grads.shape
    heads = out_weight.shape[0]
    return pl.pallas_call(
        project_kernel,
        grid=(count,),
        in_specs=[
            pl.BlockSpec((1, tok, width), lambda t: (t, 0, 0)),
            pl.BlockSpec((heads, width), lambda t: (0, t)),
        ],
        out_specs=pl.BlockSpec((tok, heads), lambda t: (0, 0)),
        out_shape=jax.ShapeDtypeStruct((tok, heads), jnp.bfloat16),
        scratch_shapes=[pltpu.VMEM((tok, heads), jnp.float32)],
        compiler_params=params(1),
        cost_estimate=pl.CostEstimate(
            flops=2 * tok * heads * width * count, bytes_accessed=16 * 2**20, transcendentals=0
        ),
        name="project_grad",
    )(grads, out_weight)


def weight_kernel(core_ref, at_ref, g_ref, out_ref, at_scr):
    @pl.when(pl.program_id(0) == 0)
    def _():
        at_scr[...] = at_ref[...].T

    out_ref[0] = mm(at_scr[...], g_ref[0], 1, 0).astype(jnp.bfloat16)


def weight_blocks(core, attn, grads, pairs):
    count, tok, width = grads.shape
    heads = attn.shape[1]
    columns = count * width // (2 * pairs)
    per = width // columns

    def pick(d, core_ref):
        block = 2 * d + core_ref[0]
        return (block // per, 0, block % per)

    return pl.pallas_call(
        weight_kernel,
        grid_spec=pltpu.PrefetchScalarGridSpec(
            num_scalar_prefetch=1,
            grid=(pairs,),
            in_specs=[
                pl.BlockSpec((tok, heads), lambda d, core_ref: (0, 0)),
                pl.BlockSpec((1, tok, columns), pick),
            ],
            out_specs=pl.BlockSpec((1, heads, columns), lambda d, core_ref: (d, 0, 0)),
            scratch_shapes=[pltpu.VMEM((heads, tok), jnp.bfloat16)],
        ),
        out_shape=jax.ShapeDtypeStruct((pairs, heads, columns), jnp.bfloat16),
        compiler_params=params(1),
        cost_estimate=pl.CostEstimate(
            flops=2 * tok * heads * columns * pairs, bytes_accessed=12 * 2**20, transcendentals=0
        ),
        name="weight_blocks",
    )(jnp.reshape(core, (1,)), attn, grads)


def local(queries, keys, values, out_weight, out_grad, doc_ids):
    tok = queries.shape[0]
    q_heads = queries.shape[1] // HEAD_SIZE
    kv_heads = keys.shape[1] // HEAD_SIZE
    factor = q_heads // kv_heads
    count = lax.axis_size("seq")
    pairs = count // 2
    shard = lax.axis_index("seq")
    core = shard % 2
    chip = shard // 2
    swap = [(s, s ^ 1) for s in range(count)]

    own = jnp.concatenate([keys, values], axis=1)
    ahead = [(s, s + 2) for s in range(count - 2)]
    to_odd = [(s, s + 1) for s in range(0, count, 2)]
    to_even = [(s + 1, s) for s in range(0, count, 2)]
    distant = lax.ppermute(own, "seq", ahead)
    from_even = lax.ppermute(own, "seq", to_odd)
    from_odd = lax.ppermute(distant, "seq", to_even)
    nearby = jnp.where(core == 1, from_even, from_odd)
    doc_far = lax.ppermute(doc_ids, "seq", ahead)
    doc_near = lax.ppermute(doc_ids, "seq", [(s, s + 1) for s in range(count - 1)])
    kv = (distant, nearby, own)
    grads = lax.all_gather(out_grad, "tensor", axis=0)

    doc_keys = jnp.concatenate([doc_far, doc_near, doc_ids])
    before = jnp.sum((doc_keys[:, None] < doc_ids[None, :]).astype(jnp.int32), axis=0)
    low = jnp.maximum(before, (2 - shard) * tok)
    low = jnp.maximum(low, jnp.arange(1, tok + 1, dtype=jnp.int32))[None, :]

    attn, lse = forward(low, queries, kv, tok, kv_heads, factor)
    sent = weight_blocks(1 - core, attn, grads, pairs)
    received = lax.ppermute(sent, "seq", swap)
    kept = weight_blocks(core, attn, grads, pairs)
    d_attn = project(grads, out_weight)

    def paired(index):
        index = jnp.clip(index, 0, pairs - 1)
        return lax.dynamic_index_in_dim(kept, index, 0, keepdims=False).astype(
            jnp.float32
        ) + lax.dynamic_index_in_dim(received, index, 0, keepdims=False).astype(jnp.float32)

    from_left = from_right = None
    for t in range(pairs - 1):
        right = paired(pairs - 1 - t + chip)
        left = paired(t - pairs + 1 + chip)
        if t:
            right = right + from_left.astype(jnp.float32)
            left = left + from_right.astype(jnp.float32)
        hops = [(2 * z + c, 2 * z + 2 + c) for z in range(t + 1) for c in range(2)]
        back = [(count - 1 - a, count - 1 - b) for a, b in hops]
        from_left = lax.ppermute(right.astype(jnp.bfloat16), "seq", hops)
        from_right = lax.ppermute(left.astype(jnp.bfloat16), "seq", back)
    weight_grad = paired(chip) + from_left.astype(jnp.float32) + from_right.astype(jnp.float32)

    dq_list = []
    totals = []
    for group in range(kv_heads):
        dq, own_part, far = backward(
            group, low, lse, queries, d_attn, attn, kv, tok, kv_heads, factor
        )
        dq_list.append(dq)
        swapped = lax.ppermute(far[tok:], "seq", swap).astype(jnp.float32)
        joined = far[:tok].astype(jnp.float32) + jnp.where(core == 1, swapped, 0.0)
        returned = lax.ppermute(
            joined.astype(jnp.bfloat16), "seq", [(s + 2, s) for s in range(count - 2)]
        )
        totals.append(
            own_part + jnp.where(core == 0, swapped, 0.0) + returned.astype(jnp.float32)
        )
    grad_queries = jnp.concatenate(dq_list, axis=1)
    grad_keys = jnp.concatenate([t[:, :HEAD_SIZE] for t in totals], axis=1)
    grad_values = jnp.concatenate([t[:, HEAD_SIZE:] for t in totals], axis=1)
    return (
        grad_queries,
        grad_keys.astype(jnp.bfloat16),
        grad_values.astype(jnp.bfloat16),
        weight_grad.astype(jnp.bfloat16),
    )


def solution(mesh):
    placed = (
        P("seq", "tensor"),
        P("seq", "tensor"),
        P("seq", "tensor"),
        P("tensor", None),
        P("seq", "tensor"),
        P("seq"),
    )
    return jax.shard_map(
        local,
        mesh=mesh,
        in_specs=placed,
        out_specs=(P("seq", "tensor"), P("seq", "tensor"), P("seq", "tensor"), P("tensor", "seq")),
        check_vma=False,
    )
```
